512 devices in a mesh: tok: 64 (over y, x, core), feat: 8 (over z).
Axes of the slice: x: 4, y: 8, z: 8, core: 2. Of those that a mesh axis runs over, the one named last changes fastest.
Arguments:
- activations: bfloat16 [131072, 8192], P('tok', 'feat'), may hold values from -200 to 200
- sketch: bfloat16 [8192, 256], P('feat'), may hold values from -0.0625 to 0.0625
Outputs:
- factor: float32 [256, 256], replicated
- projected: float32 [256, 8192], P('tok', 'feat')
The draws below stay inside these ranges and needn't reach their ends.
All inputs are finite; a program needn't handle non-finite values.
Results may differ from the reference program's by a relative error of at most 0.014.
Values may be sent and summed in bfloat16 or wider, within the bound.
No kernel may reach another device: no remote copies, remote signals or barrier semaphores. Data moves between devices by JAX's collectives and lax.ppermute only.
A program may use at most 64 MiB of HBM per device.

```python
import math
import jax
import jax.numpy as jnp
from jax import lax

D = 8192
K = 256
TOKENS = 131072
D_DEV = 1024
N_FEAT = 8


def draw_activations(key, part):
    key = jax.random.fold_in(key, 11)
    keys = jax.random.split(key, 3)
    row_scale = jnp.exp(jax.random.uniform(keys[0], (TOKENS, 1), jnp.float32, jnp.log(0.3), jnp.log(3.0)))
    ramp = 1.0 + 2.0 * jnp.arange(TOKENS, dtype=jnp.float32)[:, None] / TOKENS
    col_scale = jnp.exp(jax.random.uniform(keys[1], (1, D), jnp.float32, jnp.log(0.3), jnp.log(3.0)))
    base = jnp.clip(jax.random.normal(keys[2], (TOKENS, D), jnp.float32), -6.0, 6.0)
    return (base * row_scale * ramp * col_scale).astype(jnp.bfloat16)


def block_levels(key, shape, shards, low, largest):
    loudness, own = 1.0, jax.random.fold_in(key, 6)
    for dim, shards_of in shards:
        draws = jnp.exp(jax.random.uniform(jax.random.fold_in(own, dim), (shards_of,), jnp.float32, low / len(shards), largest / len(shards)))
        loudness = loudness * jnp.repeat(draws, shape[dim] // shards_of).reshape([-1 if axis == dim else 1 for axis in range(len(shape))])
    return loudness


def normal_values(key, extent, width, bound, cuts=(), held_as=jnp.bfloat16):
    drawn = jax.random.normal(key, extent, jnp.float32) * width
    if len(cuts) > 0:
        drawn = block_levels(key, extent, cuts, -0.22, 0.18) * drawn
    return jnp.clip(drawn, min=-bound, max=bound).astype(held_as)


def setup_inputs(seed: int = 0) -> dict:
    key_list = jax.random.split(jax.random.key(seed), 3)
    activations = draw_activations(jax.random.fold_in(key_list[2], 71), 0)
    sketch = normal_values(key_list[1], (D, K), D ** -0.5, 0.0625, ((0, 8),))
    return dict(activations=activations, sketch=sketch)


def reference(activations, sketch):
    sketch_sum = jnp.zeros((TOKENS, K), jnp.float32)
    for column_block in range(N_FEAT):
        panel_cols = activations[:, column_block * D_DEV:(column_block + 1) * D_DEV]
        product = jnp.dot(panel_cols.astype(jnp.float32), sketch[column_block * D_DEV:(column_block + 1) * D_DEV].astype(jnp.float32), preferred_element_type=jnp.float32)
        sketch_sum = sketch_sum + lax.optimization_barrier(product.astype(jnp.bfloat16)).astype(jnp.float32)
    gram_matrix = jnp.dot(sketch_sum.T.astype(jnp.float32), sketch_sum.astype(jnp.float32), precision=lax.Precision.HIGHEST, preferred_element_type=jnp.float32) / TOKENS
    lower_factor = jnp.linalg.cholesky(gram_matrix)
    basis_cols = lax.linalg.triangular_solve(lower_factor, sketch_sum.T, left_side=True, lower=True).astype(jnp.bfloat16)
    projected = jnp.dot(basis_cols.astype(jnp.float32), activations.astype(jnp.float32), preferred_element_type=jnp.float32) / math.sqrt(TOKENS)
    return (lower_factor.T, projected)
```

```python
import math

import jax
import jax.numpy as jnp
from jax import lax
from jax.sharding import Mesh, PartitionSpec as P

TOK = ("y", "x", "core")
HIGHEST = lax.Precision.HIGHEST
F32 = jnp.float32
BF16 = jnp.bfloat16


def scatter(blocks, axes):
    return lax.all_to_all(blocks, axes, 0, 0)


def gather(block, axes):
    count = lax.axis_size(axes)
    return lax.all_to_all(jnp.broadcast_to(block[None], (count,) + block.shape), axes, 0, 0)


def factorize(gram):
    lower = jnp.linalg.cholesky(gram)
    eye = jnp.eye(gram.shape[0], dtype=F32)
    inverse = lax.linalg.triangular_solve(lower, eye, left_side=True, lower=True)
    return lower.T, inverse


def shards(activations, sketch):
    tokens, features = activations.shape
    cols = sketch.shape[1]
    all_tokens = tokens * lax.axis_size(TOK)
    n_feat = lax.axis_size("feat")
    chips = lax.axis_size(("y", "x"))
    n_y = lax.axis_size("y")
    near = lax.axis_size(("x", "core"))

    partial = jnp.dot(activations, sketch, preferred_element_type=F32).astype(BF16)
    parts = scatter(partial.reshape(n_feat, tokens // n_feat, cols), "feat")
    own = jnp.sum(parts.astype(F32), axis=0)
    rows = gather(own.astype(BF16), "feat").reshape(tokens, cols)

    gram = jnp.dot(own.T, own, precision=HIGHEST, preferred_element_type=F32)
    gram = jnp.sum(scatter(gram.reshape(chips, cols // chips, cols), ("y", "x")), axis=0)
    gram = jnp.sum(gather(gram, ("core", "feat")), axis=0)
    gram = gather(gram, ("y", "x")).reshape(cols, cols) / all_tokens

    cross = jnp.dot(rows.T, activations, preferred_element_type=F32)
    cross = cross.reshape(cols, near, features // near).transpose(1, 0, 2)
    cross = jnp.sum(scatter(cross, ("x", "core")), axis=0)

    factor, inverse = factorize(gram)
    proj = jnp.dot(inverse, cross, precision=HIGHEST, preferred_element_type=F32)
    own_rows = cols // lax.axis_size(TOK)
    proj = scatter(proj.reshape(-1, own_rows, features // near), TOK)
    proj = jnp.sum(proj.reshape(n_y, near, own_rows, features // near), axis=0)
    proj = proj.transpose(1, 0, 2).reshape(own_rows, features)
    return factor, proj / math.sqrt(all_tokens)


def solution(mesh):
    n_tok, n_feat = mesh.devices.shape
    fine = Mesh(mesh.devices.reshape(n_tok // 8, 4, 2, n_feat), TOK + ("feat",))
    in_specs = (P(TOK, "feat"), P("feat", None))
    out_specs = (P(), P(TOK, "feat"))
    return jax.shard_map(shards, mesh=fine, in_specs=in_specs, out_specs=out_specs, check_vma=False)
```
